32 devices in a mesh: dp: 8 (over y, x, core), mp: 4 (over z).
Axes of the slice: x: 2, y: 2, z: 4, core: 2. Of those that a mesh axis runs over, the one named last changes fastest.
Arguments:
- feats: bfloat16 [4096, 768], P(('dp', 'mp')), may hold values from -6 to 6
- edge_owner: int32 [65536, 1], P(('dp', 'mp')), may hold values from 0 to 31; in each aligned block of 2048 rows (0 to 2047, 2048 to 4095, ...) at most 128 rows name the same one
- edge_row: int32 [65536], P(('dp', 'mp')), may hold values from 0 to 2047
- counts: int32 [4096], P(('dp', 'mp')), may hold values from 12 to 16
- table: float32 [65536, 128], P(('dp', 'mp')), may hold values from -6 to 6
- moment1: float32 [65536, 128], P(('dp', 'mp')), may hold values from -3 to 3
- moment2: float32 [65536, 128], P(('dp', 'mp')), may hold values from 0.001 to 0.1
- w_self: bfloat16 [768, 1024], replicated, may hold values from -0.21875 to 0.21875
- w_rel: bfloat16 [128, 1024], replicated, may hold values from -0.5 to 0.5
- cotangent: float32 [4096, 1024], P(('dp', 'mp')), may hold values from -6 to 6
- next_owner: int32 [4096, 1], P(('dp', 'mp')), may hold values from 0 to 31; in each aligned block of 128 rows (0 to 127, 128 to 255, ...) at most 8 rows name the same one
- next_row: int32 [4096], P(('dp', 'mp')), may hold values from 0 to 1023
- paper_table: bfloat16 [32768, 768], P(('dp', 'mp')), may hold values from -6 to 6
Outputs:
- new_table: float32 [65536, 128], P(('dp', 'mp'))
- new_moment1: float32 [65536, 128], P(('dp', 'mp'))
- new_moment2: float32 [65536, 128], P(('dp', 'mp'))
- grad_self: float32 [768, 1024], replicated
- grad_rel: float32 [128, 1024], replicated
- next_feats: bfloat16 [4096, 768], P(('dp', 'mp'))
The draws below stay inside these ranges and needn't reach their ends.
Inputs may be any that keep to these rules, and one draw needn't show every extreme that they name: `edge_owner`: in the author slots of one device at most 128 name one owner, a bound that some block reaches. `next_owner`: in the next seeds of one device at most 8 name one owner, a bound that some block reaches.
All inputs are finite; a program needn't handle non-finite values.
Results may differ from the reference program's by a relative error of at most 0.0049.
Values may be sent and summed in bfloat16 or wider, within the bound.
A program may use at most 64 MiB of HBM per device.

```python
import math
import jax
import jax.numpy as jnp
import numpy as np
from jax import lax

F = 768
E = 128
H = 1024
K = 16
S_DEV = 128
AROWS_DEV = 2048
PROWS_DEV = 1024
SEEDS = 4096
EDGES = 65536
AROWS = 65536
PROWS = 32768
CAP = 128
FCAP = 8
DEVICES = 32


def with_ends(array, stream_key, smallest, high):
    place = [jax.random.randint(jax.random.fold_in(stream_key, axis), (), 0, length) for axis, length in enumerate(array.shape)]
    main_axis = array.shape.index(max(array.shape))
    next_to = place[:main_axis] + [(place[main_axis] + 1) % array.shape[main_axis]] + place[main_axis + 1:]
    return array.at[tuple(place)].set(smallest).at[tuple(next_to)].set(high)


def levels(rng, shape, cuts, smallest, top_value):
    gain, own = 1.0, jax.random.fold_in(rng, 6)
    for axis_at, parts in cuts:
        heights = jnp.exp(jax.random.uniform(jax.random.fold_in(own, axis_at), (parts,), jnp.float32, smallest / len(cuts), top_value / len(cuts)))
        gain = gain * jnp.repeat(heights, shape[axis_at] // parts).reshape([-1 if axis == axis_at else 1 for axis in range(len(shape))])
    return gain


def assign_block(key, own, number, rows, amount, top, reach, lean):
    sequence = jax.random.permutation(key, amount)
    crowded, ordinary = shares(amount, rows * top, reach, lean, True), shares(amount, rows * top, reach, lean, False)
    places = jnp.arange(amount)

    def named(tallies, offset_by):
        used = int((tallies > 0).sum())
        fixed = max(1, used // 4)
        moved = fixed + (places - fixed + offset_by * (used - fixed)) % max(1, amount - fixed)
        return jnp.zeros((amount,), jnp.int32).at[sequence[jnp.where(places < fixed, places, moved)]].set(jnp.asarray(tallies, jnp.int32))

    tallies = jnp.where(number % 4 == 0, named(crowded, number // 4), named(ordinary, number - number // 4 - 1))
    mixed = jax.random.permutation(jax.random.fold_in(own, 3), amount)
    source_of, sink = mixed[0:amount // 2 * 2:2], mixed[1:amount // 2 * 2:2]
    room = jnp.minimum(tallies[source_of] - 1, reach - tallies[sink]) // 2
    room = jnp.where((source_of == sequence[0]) | (sink == sequence[0]) | (tallies[sink] == 0), 0, jnp.maximum(room, 0))
    moved = jax.random.randint(jax.random.fold_in(own, 4), (amount // 2,), 0, 1 << 20) % (room + 1)
    tallies = tallies.at[source_of].add(-moved).at[sink].add(moved)
    labels = jnp.searchsorted(jnp.cumsum(tallies), jnp.arange(rows * top), side="right").astype(jnp.int32)
    table = labels.reshape(top, rows).T
    table = table[jax.random.permutation(jax.random.fold_in(own, 1), rows)]
    offset_by = jax.random.randint(jax.random.fold_in(own, 2), (rows, 1), 0, top)
    return jnp.take_along_axis(table, (jnp.arange(top)[None, :] + offset_by) % top, axis=1)


def shares(amount, total, limit, lean, full):
    portions = [(1 << 20) // math.isqrt(rank ** lean) + 1 for rank in range(1, amount + 1)]
    largest = limit if full else min(limit, max(-(-total // amount), total * portions[0] // sum(portions)))
    least = 1 if total - largest >= amount - 1 else 0
    given, surplus = [largest] + [least] * (amount - 1), total - largest - least * (amount - 1)
    while surplus > 0:
        movable = [i for i in range(1, amount) if given[i] < largest] or [i for i in range(1, amount) if given[i] < limit]
        pool, left = sum([portions[i] for i in movable]), surplus
        for i in movable:
            more = min(limit - given[i], max(1, left * portions[i] // pool), surplus)
            given[i] = given[i] + more
            surplus = surplus - more
    return np.array(given)


def normal_values(rng, extent, spread, reach, pieces=(), held_as=jnp.bfloat16):
    values = jax.random.normal(rng, extent, jnp.float32) * spread
    if len(pieces) > 0:
        values = levels(rng, extent, pieces, -0.22, 0.18) * values
    return jnp.clip(values, min=-reach, max=reach).astype(held_as)


def setup_inputs(seed: int = 0) -> dict:
    key_list = jax.random.split(jax.random.key(seed), 14)
    feats = normal_values(key_list[0], (SEEDS, F), 1.0, 6.0, ((0, 32),))
    edge_owner_keys = jax.random.split(jax.random.fold_in(key_list[1], 1), EDGES // (S_DEV * K))
    edge_owner_turns = jax.random.permutation(jax.random.fold_in(key_list[1], 3), EDGES // (S_DEV * K))
    edge_owner = jax.vmap(lambda own, number: assign_block(jax.random.fold_in(key_list[1], 2), own, number, S_DEV * K, DEVICES, 1, CAP, 2))(edge_owner_keys, edge_owner_turns).reshape((EDGES, 1))
    edge_row = with_ends(jax.random.randint(key_list[2], (EDGES,), 0, AROWS_DEV), jax.random.fold_in(key_list[2], 1), 0, AROWS_DEV - 1).astype(jnp.int32)
    counts = with_ends(jax.random.randint(key_list[3], (SEEDS,), K - K // 4, K + 1), jax.random.fold_in(key_list[3], 1), K - K // 4, K).astype(jnp.int32)
    table = normal_values(key_list[4], (AROWS, E), 1.0, 6.0, ((0, 32),), jnp.float32)
    moment1 = normal_values(key_list[5], (AROWS, E), 0.2, 3.0, ((0, 32),), jnp.float32)
    moment2 = jnp.clip(jnp.exp(math.log(0.1) - 4.6051702 * jax.random.uniform(key_list[6], (AROWS, E), jnp.float32) ** levels(key_list[6], (AROWS, E), ((0, 32),), -0.2, 0.2)), 0.001, 0.1)
    w_self = normal_values(key_list[7], (F, H), F ** -0.5, 0.21875)
    w_rel = normal_values(key_list[8], (E, H), E ** -0.5, 0.5)
    cotangent = normal_values(key_list[9], (SEEDS, H), 1.0, 6.0, ((0, 32),), jnp.float32)
    next_owner_keys = jax.random.split(jax.random.fold_in(key_list[10], 1), SEEDS // S_DEV)
    next_owner_turns = jax.random.permutation(jax.random.fold_in(key_list[10], 3), SEEDS // S_DEV)
    next_owner = jax.vmap(lambda own, number: assign_block(jax.random.fold_in(key_list[10], 2), own, number, S_DEV, DEVICES, 1, FCAP, 2))(next_owner_keys, next_owner_turns).reshape((SEEDS, 1))
    next_row = with_ends(jax.random.randint(key_list[11], (SEEDS,), 0, PROWS_DEV), jax.random.fold_in(key_list[11], 1), 0, PROWS_DEV - 1).astype(jnp.int32)
    paper_table = normal_values(key_list[12], (PROWS, F), 1.0, 6.0, ((0, 32),))
    return {"feats": feats, "edge_owner": edge_owner, "edge_row": edge_row, "counts": counts, "table": table, "moment1": moment1, "moment2": moment2, "w_self": w_self, "w_rel": w_rel, "cotangent": cotangent, "next_owner": next_owner, "next_row": next_row, "paper_table": paper_table}


def reference(feats, edge_owner, edge_row, counts, table, moment1, moment2, w_self, w_rel, cotangent, next_owner, next_row, paper_table):
    author_id = edge_owner[:, 0].astype(jnp.int32) * AROWS_DEV + edge_row
    live = jnp.arange(K, dtype=jnp.int32)[None, :] < counts[:, None]
    count_f = counts.astype(jnp.float32)
    edge_vals = jnp.take(table, author_id, axis=0).reshape(SEEDS, K, E)
    agg = lax.optimization_barrier(jnp.sum(jnp.where(live[:, :, None], edge_vals, jnp.float32(0.0)), axis=1)) / count_f[:, None]
    agg_b = agg.astype(jnp.bfloat16)
    pre = jnp.dot(feats, w_self, preferred_element_type=jnp.float32) + jnp.dot(agg_b, w_rel, preferred_element_type=jnp.float32)
    sig = jax.nn.sigmoid(pre)
    dpre = (cotangent * sig * (1.0 + pre * (1.0 - sig))).astype(jnp.bfloat16)
    grad_self = jnp.dot(feats.T, dpre, preferred_element_type=jnp.float32)
    grad_rel = jnp.dot(agg_b.T, dpre, preferred_element_type=jnp.float32)
    dagg = jnp.dot(dpre, w_rel.T, preferred_element_type=jnp.float32)
    slot_grad = jnp.where(live[:, :, None], (dagg / count_f[:, None])[:, None, :], jnp.float32(0.0)).reshape(SEEDS * K, E)
    row_grad = jax.ops.segment_sum(slot_grad, author_id, num_segments=AROWS)
    hits = jax.ops.segment_sum(live.reshape(-1).astype(jnp.int32), author_id, num_segments=AROWS)
    touched = (hits > 0)[:, None]
    m_new = 0.9 * moment1 + 0.1 * row_grad
    v_new = 0.999 * moment2 + 0.001 * row_grad * row_grad
    step = 0.05 * (m_new / (1.0 - 0.9 ** 10)) / (jnp.sqrt(v_new / (1.0 - 0.999 ** 10)) + 1e-08)
    new_table = jnp.where(touched, table - step, table)
    new_moment1 = jnp.where(touched, m_new, moment1)
    new_moment2 = jnp.where(touched, v_new, moment2)
    paper_id = next_owner[:, 0].astype(jnp.int32) * PROWS_DEV + next_row
    next_feats = jnp.take(paper_table, paper_id, axis=0)
    return (new_table, new_moment1, new_moment2, grad_self, grad_rel, next_feats)
```

```python
import functools

import jax
import jax.numpy as jnp
from jax import lax
from jax.experimental import pallas as pl
from jax.experimental.pallas import tpu as pltpu
from jax.sharding import PartitionSpec as P

F32, BF16, I32 = jnp.float32, jnp.bfloat16, jnp.int32
LANES = 128
VMEM_LIMIT = 48 * 1024 * 1024
MESH = pl.DeviceIdType.MESH
VM = pl.BlockSpec(memory_space=pltpu.VMEM)


def dot_nt(a, b):
    return lax.dot_general(a, b, (((1,), (1,)), ((), ())), preferred_element_type=F32)


def dot_nn(a, b):
    return jnp.dot(a, b, preferred_element_type=F32)


def split(x):
    hi = x.astype(BF16)
    return hi, (x - hi.astype(F32)).astype(BF16)


def onehot(mask):
    return jnp.where(mask, 1.0, 0.0).astype(BF16)


def steps_of(n_dp, n_mp):
    return [(0, 1 << b) for b in range(n_dp.bit_length() - 1)] + [
        (1, 1 << b) for b in range(n_mp.bit_length() - 1)
    ]


def position_of(device, n_mp, steps):
    coords = (device // n_mp, device % n_mp)
    pos = 0
    for axis, w in steps:
        pos = pos * 2 + (coords[axis] // w) % 2
    return pos


def partners(steps):
    coords = (lax.axis_index("dp"), lax.axis_index("mp"))
    found = []
    for axis, w in steps:
        bit = lax.rem(coords[axis] // w, 2)
        other = coords[axis] + w * (1 - 2 * bit)
        found.append((bit, (other, coords[1]) if axis == 0 else (coords[0], other)))
    return found


def enter(found):
    barrier = pltpu.get_barrier_semaphore()
    for _, device in found:
        pl.semaphore_signal(barrier, inc=1, device_id=device, device_id_type=MESH)
    pl.semaphore_wait(barrier, len(found))


def rs_scratch(n, block, wires):
    shapes = []
    for s, wire in enumerate(wires):
        half = n >> (s + 1)
        shapes += [pltpu.VMEM((half, *block), wire), pltpu.VMEM((half, *block), F32)]
        shapes += [pltpu.VMEM((half, *block) if wire == BF16 else (1, 8, LANES), wire)]
    return shapes


def rs_start(cur, scratch, s, n, wire, bit, device, send, recv):
    half = n >> (s + 1)
    arrive, _, rounded = scratch[3 * s : 3 * s + 3]
    away = (1 - bit) * half
    if wire == BF16:

        @pl.loop(0, half)
        def _(i):
            rounded[i] = cur[away + i].astype(BF16)

        src = rounded
    else:
        src = cur.at[pl.ds(away, half)]
    copy = pltpu.make_async_remote_copy(
        src_ref=src, dst_ref=arrive, send_sem=send.at[s], recv_sem=recv.at[s],
        device_id=device, device_id_type=MESH,
    )
    copy.start()
    return copy


def rs_add(cur, scratch, s, n, bit):
    half = n >> (s + 1)
    arrive, total, _ = scratch[3 * s : 3 * s + 3]

    @pl.loop(0, half)
    def _(i):
        total[i] = cur[bit * half + i] + arrive[i].astype(F32)

    return total


def ag_start(out, s, n, pos, device, send, recv):
    size = n >> (s + 1)
    here = out.at[pl.ds((pos // size) * size, size)]
    copy = pltpu.make_async_remote_copy(
        src_ref=here, dst_ref=here, send_sem=send.at[s], recv_sem=recv.at[s],
        device_id=device, device_id_type=MESH,
    )
    copy.start()
    return copy


def my_position(found):
    pos = 0
    for bit, _ in found:
        pos = pos * 2 + bit
    return pos


def reduce_kernel(n, steps, wires, x, out, *rest):
    scratch, (send, recv) = rest[:-2], rest[-2:]
    found = partners(steps)
    enter(found)
    cur = x
    for s, (bit, device) in enumerate(found):
        rs_start(cur, scratch, s, n, wires[s], bit, device, send, recv).wait()
        cur = rs_add(cur, scratch, s, n, bit)
    out[...] = cur[0]


def exchange_kernel(n, steps, wires, grads, dagg, out_dagg, out_grads, *rest):
    scratch, (send, recv, gsend, grecv, hsend, hrecv) = rest[:-6], rest[-6:]
    found = partners(steps)
    pos = my_position(found)
    enter(found)
    out_dagg[pos] = dagg[...]
    cur = grads
    last = len(steps) - 1
    for s, (bit, device) in enumerate(found):
        first = rs_start(cur, scratch, s, n, wires[s], bit, device, send, recv)
        second = ag_start(out_dagg, last - s, n, pos, found[last - s][1], gsend, grecv)
        first.wait()
        cur = rs_add(cur, scratch, s, n, bit)
        second.wait()
    out_grads[pos] = cur[0].astype(BF16)
    for s in reversed(range(len(steps))):
        ag_start(out_grads, s, n, pos, found[s][1], hsend, hrecv).wait()


def place_kernel(n, cap, slots_per, owner, row, counts, out_row, out_seed):
    blocks = owner.shape[0]
    seeds = counts.shape[1]
    per = LANES // slots_per
    at_seed = lax.broadcasted_iota(I32, (blocks, seeds), 1)
    at_block = lax.broadcasted_iota(I32, (blocks, seeds), 0)
    spread = jnp.where(at_seed // per == at_block, counts[...].astype(F32), 0.0).astype(BF16)
    s_i = lax.broadcasted_iota(I32, (seeds, LANES), 0)
    l_i = lax.broadcasted_iota(I32, (seeds, LANES), 1)
    count = dot_nn(spread, onehot(lax.rem(s_i, per) == l_i // slots_per))
    lane = lax.broadcasted_iota(I32, (blocks, LANES), 1)
    live = lax.rem(lane, slots_per).astype(F32) < count - 0.5
    wanted = jnp.where(live, row[...] + 1, 0)
    seed = lax.broadcasted_iota(I32, (blocks, LANES), 0) * per + lane // slots_per
    parts = [(wanted // 64).astype(F32), lax.rem(wanted, 64).astype(F32), seed.astype(F32)]
    dev = lax.broadcasted_iota(I32, (n, LANES), 0)
    hot = [jnp.where(dev == owner[a : a + 1, :], 1.0, 0.0) for a in range(blocks)]
    t_i = lax.broadcasted_iota(I32, (LANES, LANES), 0)
    t_j = lax.broadcasted_iota(I32, (LANES, LANES), 1)
    before = dot_nn(jnp.concatenate([h.astype(BF16) for h in hot], axis=0), onehot(t_i < t_j))
    base = jnp.zeros((n, 1), F32)
    place = lax.broadcasted_iota(I32, (cap, LANES), 0).astype(F32)
    left, right = [], []
    for a in range(blocks):
        slot = jnp.sum(hot[a] * (before[a * n : (a + 1) * n] + base), axis=0, keepdims=True)
        base = base + jnp.sum(hot[a], axis=1, keepdims=True)
        right.append(onehot(place == slot))
        left.append(
            jnp.concatenate([(hot[a] * p[a : a + 1, :]).astype(BF16) for p in parts], axis=0)
        )
    got = dot_nt(jnp.concatenate(left, axis=1), jnp.concatenate(right, axis=1))
    out_row[...] = (got[:n] * 64.0 + got[n : 2 * n] - 1.0).astype(I32)
    out_seed[...] = got[2 * n :].astype(I32)


def seed_hot(seed, d, cap, seeds):
    q = LANES // cap
    lane = lax.broadcasted_iota(I32, (1, LANES), 1)
    which = seed[pl.ds(d, 1), :] + seeds * (lane // cap)
    return onehot(lax.broadcasted_iota(I32, (q * seeds, LANES), 0) == which)


def fetch_kernel(cap, places, rows, seed, table, out, packed):
    n_rows, emb = table.shape
    seeds = out.shape[2]
    q = LANES // cap
    flipped = table[...].T
    hi, lo = split(flipped)
    packed[:emb, :] = hi
    packed[emb:, :] = lo
    at = lax.broadcasted_iota(I32, (n_rows, LANES), 0)
    for d in range(0, rows.shape[0], 2):
        hot = jnp.concatenate([onehot(at == rows[d + j : d + j + 1, :]) for j in range(2)], axis=1)
        got = dot_nn(packed[...], hot)
        vals = got[:emb] + got[emb:]
        for j in range(2):
            v_hi, v_lo = split(vals[:, j * LANES : (j + 1) * LANES])
            both = dot_nt(jnp.concatenate([v_hi, v_lo], axis=0), seed_hot(seed, d + j, cap, seeds))
            sums = both[:emb] + both[emb:]
            for k in range(q):
                out[places[(d + j) * q + k]] = sums[:, k * seeds : (k + 1) * seeds]


def layer_kernel(agg_sum, counts, feats, w_self, w_rel, cot, out_parts, out_dagg):
    n, rows, _ = out_parts.shape
    width = w_self.shape[1]
    tiles = width // LANES
    count = counts[...].astype(F32)
    agg_t = agg_sum[...] / count
    agg_b = agg_t.T.astype(BF16)
    pre = dot_nn(feats[...], w_self[...]) + dot_nn(agg_b, w_rel[...])
    sig = 1.0 / (1.0 + jnp.exp(-pre))
    dpre = (cot[...] * sig * (1.0 + pre * (1.0 - sig))).astype(BF16)
    out_dagg[...] = (dot_nt(w_rel[...], dpre) / count).astype(BF16)
    flipped = [feats[...].astype(F32).T.astype(BF16), agg_t.astype(BF16)]
    pad = n // tiles * rows - flipped[0].shape[0] - flipped[1].shape[0]
    if pad:
        flipped.append(jnp.zeros((pad, agg_t.shape[1]), BF16))
    lhs = jnp.concatenate(flipped, axis=0)
    for i in range(n // tiles):
        got = dot_nn(lhs[i * rows : (i + 1) * rows], dpre)
        for t in range(tiles):
            out_parts[i * tiles + t] = got[:, t * LANES : (t + 1) * LANES]


def adam_kernel(cap, places, rows, seed, dagg, table, m1, m2, o_table, o_m1, o_m2, slot_g, hot):
    size, emb = table.shape
    seeds = dagg.shape[2]
    q = LANES // cap
    blocks = rows.shape[0]

    @pl.when(pl.program_id(0) == 0)
    def _():
        for d in range(blocks):
            grads = [dagg[places[d * q + k]] for k in range(q)]
            got = dot_nn(jnp.concatenate(grads, axis=1), seed_hot(seed, d, cap, seeds))
            slot_g[:emb, d * LANES : (d + 1) * LANES] = got.astype(BF16)
        slot_g[emb:, :] = jnp.ones((emb, blocks * LANES), BF16)

    at = lax.broadcasted_iota(I32, (size, LANES), 0) + pl.program_id(0) * size
    for d in range(blocks):
        hot[:, d * LANES : (d + 1) * LANES] = onehot(at == rows[d : d + 1, :])
    got = dot_nt(hot[...], slot_g[...])
    grad, touched = got[:, :emb], got[:, emb:] > 0.5
    m_new = 0.9 * m1[...] + 0.1 * grad
    v_new = 0.999 * m2[...] + 0.001 * grad * grad
    step = 0.05 * (m_new / (1.0 - 0.9**10)) / (jnp.sqrt(v_new / (1.0 - 0.999**10)) + 1e-08)
    o_table[...] = jnp.where(touched, table[...] - step, table[...])
    o_m1[...] = jnp.where(touched, m_new, m1[...])
    o_m2[...] = jnp.where(touched, v_new, m2[...])


def params(**more):
    return pltpu.CompilerParams(vmem_limit_bytes=VMEM_LIMIT, **more)


def place_slots(owner, capacity, count_dev):
    owner_col = owner[:, 0]
    hot = (owner_col[:, None] == jnp.arange(count_dev, dtype=I32)[None, :]).astype(I32)
    before = jnp.cumsum(hot, axis=0) - hot
    return owner_col * capacity + jnp.sum(before * hot, axis=1)


def all_to_all(x):
    return lax.all_to_all(x, ("dp", "mp"), split_axis=0, concat_axis=0, tiled=True)


def shards(
    feats,
    edge_owner,
    edge_row,
    counts,
    table,
    moment1,
    moment2,
    w_self,
    w_rel,
    cotangent,
    next_owner,
    next_row,
    paper_table,
):
    n_dp, n_mp = lax.axis_size("dp"), lax.axis_size("mp")
    n = n_dp * n_mp
    steps = steps_of(n_dp, n_mp)
    places = [position_of(d, n_mp, steps) for d in range(n)]
    seeds = counts.shape[0]
    edges = edge_row.shape[0]
    n_rows, emb = table.shape
    feat_w, hidden = w_self.shape
    width = paper_table.shape[1]
    cap = max(2, 2 * edges // n)
    fcap = max(2, 2 * seeds // n)
    blocks = n * cap // LANES
    counts_row = counts.reshape(1, seeds)

    asked_row, asked_seed = pl.pallas_call(
        functools.partial(place_kernel, n, cap, edges // seeds),
        out_shape=[jax.ShapeDtypeStruct((n, cap), I32)] * 2,
        in_specs=[VM] * 3,
        out_specs=[VM] * 2,
        compiler_params=params(),
        name="place",
    )(edge_owner.reshape(edges // LANES, LANES), edge_row.reshape(edges // LANES, LANES), counts_row)

    paper_place = place_slots(next_owner, fcap, n)
    paper_asked = jnp.zeros((n * fcap,), I32).at[paper_place].set(next_row).reshape(n, fcap)
    wanted = all_to_all(jnp.concatenate([asked_row, asked_seed, paper_asked], axis=1))
    rows = wanted[:, :cap].reshape(blocks, LANES)
    slot_seed = wanted[:, cap : 2 * cap].reshape(blocks, LANES)
    paper_rows = all_to_all(jnp.take(paper_table, wanted[:, 2 * cap :], axis=0, mode="clip"))
    next_feats = jnp.take(paper_rows.reshape(n * fcap, width), paper_place, axis=0, mode="clip")

    partial_agg = pl.pallas_call(
        functools.partial(fetch_kernel, cap, places),
        out_shape=jax.ShapeDtypeStruct((n, emb, seeds), F32),
        in_specs=[VM] * 3,
        out_specs=VM,
        scratch_shapes=[pltpu.VMEM((2 * emb, n_rows), BF16)],
        compiler_params=params(),
        name="fetch",
    )(rows, slot_seed, table)

    sems = [pltpu.SemaphoreType.DMA((len(steps),)) for _ in range(2)]
    wires = [BF16 if (axis, w) == (0, 2) else F32 for axis, w in steps]
    agg_sum = pl.pallas_call(
        functools.partial(reduce_kernel, n, steps, wires),
        out_shape=jax.ShapeDtypeStruct((emb, seeds), F32),
        in_specs=[VM],
        out_specs=VM,
        scratch_shapes=rs_scratch(n, (emb, seeds), wires) + sems,
        compiler_params=params(collective_id=1, has_side_effects=True),
        name="sum_agg",
    )(partial_agg)

    tiles = hidden // LANES
    chunk = -(-(feat_w + emb) * tiles // (n * 16)) * 16
    parts, dagg = pl.pallas_call(
        layer_kernel,
        out_shape=[
            jax.ShapeDtypeStruct((n, chunk, LANES), F32),
            jax.ShapeDtypeStruct((emb, seeds), BF16),
        ],
        in_specs=[VM] * 6,
        out_specs=[VM] * 2,
        compiler_params=params(),
        name="layer",
    )(agg_sum, counts_row, feats, w_self, w_rel, cotangent)

    wires = [BF16 if axis == 0 and w > 1 else F32 for axis, w in steps]
    all_dagg, grads = pl.pallas_call(
        functools.partial(exchange_kernel, n, steps, wires),
        out_shape=[
            jax.ShapeDtypeStruct((n, emb, seeds), BF16),
            jax.ShapeDtypeStruct((n, chunk, LANES), BF16),
        ],
        in_specs=[VM] * 2,
        out_specs=[VM] * 2,
        scratch_shapes=rs_scratch(n, (chunk, LANES), wires) + sems * 3,
        compiler_params=params(collective_id=2, has_side_effects=True),
        name="exchange",
    )(parts, dagg)
    grads = grads.reshape(n // tiles, tiles, chunk, LANES).transpose(0, 2, 1, 3)
    grads = grads.reshape(n // tiles * chunk, hidden).astype(F32)
    grad_self, grad_rel = grads[:feat_w], grads[feat_w : feat_w + emb]

    size = min(256, n_rows)
    whole = lambda shape: pl.BlockSpec(shape, lambda i: (0,) * len(shape))
    by_row = pl.BlockSpec((size, emb), lambda i: (i, 0))
    new_table, new_moment1, new_moment2 = pl.pallas_call(
        functools.partial(adam_kernel, cap, places),
        out_shape=[jax.ShapeDtypeStruct((n_rows, emb), F32)] * 3,
        grid=(n_rows // size,),
        in_specs=[whole((blocks, LANES))] * 2 + [whole((n, emb, seeds))] + [by_row] * 3,
        out_specs=[by_row] * 3,
        scratch_shapes=[
            pltpu.VMEM((2 * emb, blocks * LANES), BF16),
            pltpu.VMEM((size, blocks * LANES), BF16),
        ],
        compiler_params=params(),
        name="adam",
    )(rows, slot_seed, all_dagg, table, moment1, moment2)
    return (new_table, new_moment1, new_moment2, grad_self, grad_rel, next_feats)


def solution(mesh):
    both = P(("dp", "mp"), None)
    flat = P(("dp", "mp"))
    in_specs = (both, both, flat, flat, both, both, both, P(), P(), both, both, flat, both)
    out_specs = (both, both, both, P(), P(), both)
    return jax.shard_map(shards, mesh=mesh, in_specs=in_specs, out_specs=out_specs, check_vma=False)
```

```python
import functools

import jax
import jax.numpy as jnp
from jax import lax
from jax.experimental import pallas as pl
from jax.experimental.pallas import tpu as pltpu
from jax.sharding import PartitionSpec as P

F32, BF16, I32 = jnp.float32, jnp.bfloat16, jnp.int32
LANES = 128
VMEM_LIMIT = 48 * 1024 * 1024
MESH = pl.DeviceIdType.MESH
VM = pl.BlockSpec(memory_space=pltpu.VMEM)


def dot_nt(a, b):
    return lax.dot_general(a, b, (((1,), (1,)), ((), ())), preferred_element_type=F32)


def dot_nn(a, b):
    return jnp.dot(a, b, preferred_element_type=F32)


def split(x):
    hi = x.astype(BF16)
    return hi, (x - hi.astype(F32)).astype(BF16)


def onehot(mask):
    return jnp.where(mask, 1.0, 0.0).astype(BF16)


def orders_of(n_dp, n_mp):
    core, *chips = [(0, 1 << b) for b in range(n_dp.bit_length() - 1)]
    lines = [(1, 1 << b) for b in range(n_mp.bit_length() - 1)]
    h = len(chips) // 2
    return [core, *chips, *lines], [core, *chips[h:], *chips[:h], *lines]


def position_of(device, n_mp, steps):
    coords = (device // n_mp, device % n_mp)
    pos = 0
    for axis, w in steps:
        pos = pos * 2 + (coords[axis] // w) % 2
    return pos


def partners(steps):
    coords = (lax.axis_index("dp"), lax.axis_index("mp"))
    found = []
    for axis, w in steps:
        bit = lax.rem(coords[axis] // w, 2)
        other = coords[axis] + w * (1 - 2 * bit)
        found.append((bit, (other, coords[1]) if axis == 0 else (coords[0], other)))
    return found


def enter(found):
    barrier = pltpu.get_barrier_semaphore()
    for _, device in found:
        pl.semaphore_signal(barrier, inc=1, device_id=device, device_id_type=MESH)
    pl.semaphore_wait(barrier, len(found))


def my_position(found):
    pos = 0
    for bit, _ in found:
        pos = pos * 2 + bit
    return pos


def pieces_of(rows, count):
    groups, at, found = rows // 16, 0, []
    for i in range(count):
        size = (groups // count + (i < groups % count)) * 16
        found.append((at, size))
        at += size
    return found


def sems(steps):
    return [pltpu.SemaphoreType.DMA((len(steps),)) for _ in range(2)]


def rs_scratch(n, block, steps, narrow):
    shapes = sems(steps)
    for s, step in enumerate(steps):
        half = n >> (s + 1)
        shapes += [pltpu.VMEM((half, *block), BF16 if narrow(step) else F32)]
        shapes += [pltpu.VMEM((half, *block), F32)]
        shapes += [pltpu.VMEM((half, *block) if narrow(step) else (1, 16, LANES), BF16)]
    return shapes


def rs_chain(x, n, steps, found, narrow, scratch):
    send, recv = scratch[:2]
    cur = x
    for s, (bit, device) in enumerate(found):
        half = n >> (s + 1)
        arrive, total, rounded = scratch[2 + 3 * s : 5 + 3 * s]
        away, keep = (1 - bit) * half, bit * half
        src = cur.at[pl.ds(away, half)]
        if narrow(steps[s]):
            src = rounded

            @pl.loop(0, half)
            def _(i, cur=cur, rounded=rounded, away=away):
                rounded[i] = cur[away + i].astype(BF16)

        copy = pltpu.make_async_remote_copy(
            src_ref=src, dst_ref=arrive, send_sem=send.at[s], recv_sem=recv.at[s],
            device_id=device, device_id_type=MESH,
        )
        copy.start()
        yield
        copy.wait()

        @pl.loop(0, half)
        def _(i, cur=cur, total=total, arrive=arrive, keep=keep):
            total[i] = cur[keep + i] + arrive[i].astype(F32)

        cur = total
    return cur


def ag_chain(out, n, found, scratch):
    send, recv = scratch
    pos = my_position(found)
    for s in reversed(range(len(found))):
        size = n >> (s + 1)
        here = out.at[pl.ds((pos // size) * size, size)]
        copy = pltpu.make_async_remote_copy(
            src_ref=here, dst_ref=here, send_sem=send.at[s], recv_sem=recv.at[s],
            device_id=found[s][1], device_id_type=MESH,
        )
        copy.start()
        yield
        copy.wait()


def run(chains):
    while chains:
        left = []
        for chain in chains:
            try:
                next(chain)
                left.append(chain)
            except StopIteration:
                pass
        chains = left


def reduce_kernel(n, orders, narrow, xs, out, *scratch):
    found = [partners(steps) for steps in orders]
    enter(found[0])
    per = len(scratch) // len(xs)
    starts = [0]
    for x in xs:
        starts.append(starts[-1] + x.shape[1])

    def chain(k):
        mine = scratch[k * per : (k + 1) * per]
        total = yield from rs_chain(xs[k], n, orders[k % 2], found[k % 2], narrow, mine)
        out[starts[k] : starts[k + 1], :] = total[0]

    run([chain(k) for k in range(len(xs))])


def exchange_kernel(n, orders, narrow, parts, daggs, out_daggs, out_grads, *scratch):
    found = [partners(steps) for steps in orders]
    pos = [my_position(f) for f in found]
    enter(found[0])
    count, small = len(parts), 2 * len(daggs)
    mine, rest = scratch[:small], scratch[small:]
    per = len(rest) // count

    def row_chain(k):
        out_daggs[k][pos[k % 2]] = daggs[k][...]
        yield from ag_chain(out_daggs[k], n, found[k % 2], mine[2 * k : 2 * k + 2])

    def grad_chain(k):
        own = rest[k * per : (k + 1) * per]
        total = yield from rs_chain(parts[k], n, orders[k % 2], found[k % 2], narrow, own[2:])
        out_grads[k][pos[k % 2]] = total[0].astype(BF16)
        yield from ag_chain(out_grads[k], n, found[k % 2], own[:2])

    run([grad_chain(k) for k in range(count)] + [row_chain(k) for k in range(len(daggs))])


def place_kernel(
    n, cap, fcap, slots_per, owner, row, counts, p_owner, p_row, out_row, out_seed, out_asked, out_place
):
    blocks = owner.shape[0]
    seeds = counts.shape[1]
    per = LANES // slots_per
    at_seed = lax.broadcasted_iota(I32, (blocks, seeds), 1)
    at_block = lax.broadcasted_iota(I32, (blocks, seeds), 0)
    spread = jnp.where(at_seed // per == at_block, counts[...].astype(F32), 0.0).astype(BF16)
    s_i = lax.broadcasted_iota(I32, (seeds, LANES), 0)
    l_i = lax.broadcasted_iota(I32, (seeds, LANES), 1)
    count = dot_nn(spread, onehot(lax.rem(s_i, per) == l_i // slots_per))
    lane = lax.broadcasted_iota(I32, (blocks, LANES), 1)
    live = lax.rem(lane, slots_per).astype(F32) < count - 0.5
    wanted = jnp.where(live, row[...] + 1, 0)
    seed = lax.broadcasted_iota(I32, (blocks, LANES), 0) * per + lane // slots_per
    parts = [(wanted // 64).astype(F32), lax.rem(wanted, 64).astype(F32), seed.astype(F32)]
    dev = lax.broadcasted_iota(I32, (n, LANES), 0)
    hot = [jnp.where(dev == owner[a : a + 1, :], 1.0, 0.0) for a in range(blocks)]
    t_i = lax.broadcasted_iota(I32, (LANES, LANES), 0)
    t_j = lax.broadcasted_iota(I32, (LANES, LANES), 1)
    before = dot_nn(jnp.concatenate([h.astype(BF16) for h in hot], axis=0), onehot(t_i < t_j))
    base = jnp.zeros((n, 1), F32)
    place = lax.broadcasted_iota(I32, (cap, LANES), 0).astype(F32)
    left, right = [], []
    for a in range(blocks):
        slot = jnp.sum(hot[a] * (before[a * n : (a + 1) * n] + base), axis=0, keepdims=True)
        base = base + jnp.sum(hot[a], axis=1, keepdims=True)
        right.append(onehot(place == slot))
        left.append(
            jnp.concatenate([(hot[a] * p[a : a + 1, :]).astype(BF16) for p in parts], axis=0)
        )
    got = dot_nt(jnp.concatenate(left, axis=1), jnp.concatenate(right, axis=1))
    out_row[...] = (got[:n] * 64.0 + got[n : 2 * n] - 1.0).astype(I32)
    out_seed[...] = got[2 * n :].astype(I32)
    p_hot = jnp.where(dev == p_owner[...], 1.0, 0.0)
    slot = jnp.sum(p_hot * dot_nn(p_hot.astype(BF16), onehot(t_i < t_j)), axis=0, keepdims=True)
    out_place[...] = p_owner[...] * fcap + slot.astype(I32)
    high, low = p_row[...] // 64, lax.rem(p_row[...], 64)
    pair = [(p_hot * v.astype(F32)).astype(BF16) for v in (high, low)]
    at_slot = onehot(lax.broadcasted_iota(I32, (fcap, LANES), 0).astype(F32) == slot)
    got = dot_nt(jnp.concatenate(pair, axis=0), at_slot)
    out_asked[...] = (got[:n] * 64.0 + got[n:]).astype(I32)


def pick(rows, wanted):
    at = lax.broadcasted_iota(I32, (rows.shape[0], LANES), 0)
    got = [
        lax.dot_general(
            onehot(at == wanted[i : i + 1, :]), rows, (((0,), (0,)), ((), ())),
            preferred_element_type=F32,
        )
        for i in range(wanted.shape[0])
    ]
    return jnp.concatenate(got, axis=0).astype(BF16)


def papers_kernel(wanted, papers, out):
    out[...] = pick(papers[...], wanted)


def unpack_kernel(pieces, tiles, grads, place, rows, out_self, out_rel, out_next):
    out_next[...] = pick(rows[...], place)
    chunk = sum(size for _, size in pieces)
    for (start, size), grad in zip(pieces, grads):
        for j in range(grad.shape[0]):
            top = j // tiles * chunk + start
            cols = slice(j % tiles * LANES, (j % tiles + 1) * LANES)
            first = 0
            for out in (out_self, out_rel):
                low, high = max(top, first), min(top + size, first + out.shape[0])
                if low < high:
                    out[low - first : high - first, cols] = grad[j, low - top : high - top].astype(F32)
                first += out.shape[0]


def seed_hot(seed, d, cap, seeds):
    q = LANES // cap
    lane = lax.broadcasted_iota(I32, (1, LANES), 1)
    which = seed[pl.ds(d, 1), :] + seeds * (lane // cap)
    return onehot(lax.broadcasted_iota(I32, (q * seeds, LANES), 0) == which)


def fetch_kernel(cap, places, rows, seed, table, outs, packed):
    n_rows, emb = table.shape
    seeds = outs[0].shape[2]
    q = LANES // cap
    flipped = table[...].T
    hi, lo = split(flipped)
    packed[:emb, :] = hi
    packed[emb:, :] = lo
    at = lax.broadcasted_iota(I32, (n_rows, LANES), 0)
    for d in range(0, rows.shape[0], 2):
        hot = jnp.concatenate([onehot(at == rows[d + j : d + j + 1, :]) for j in range(2)], axis=1)
        got = dot_nn(packed[...], hot)
        vals = got[:emb] + got[emb:]
        for j in range(2):
            v_hi, v_lo = split(vals[:, j * LANES : (j + 1) * LANES])
            both = dot_nt(jnp.concatenate([v_hi, v_lo], axis=0), seed_hot(seed, d + j, cap, seeds))
            sums = both[:emb] + both[emb:]
            for k in range(q):
                at_row = 0
                for p, out in enumerate(outs):
                    size = out.shape[1]
                    place = places[p % 2][(d + j) * q + k]
                    out[place] = sums[at_row : at_row + size, k * seeds : (k + 1) * seeds]
                    at_row += size


def layer_kernel(agg_sum, counts, feats, w_self, w_rel, cot, out_parts, out_daggs):
    n = out_parts[0].shape[0]
    rows = sum(out.shape[1] for out in out_parts)
    width = w_self.shape[1]
    tiles = width // LANES
    count = counts[...].astype(F32)
    agg_t = agg_sum[...] / count
    agg_b = agg_t.T.astype(BF16)
    pre = dot_nn(feats[...], w_self[...]) + dot_nn(agg_b, w_rel[...])
    sig = 1.0 / (1.0 + jnp.exp(-pre))
    dpre = (cot[...] * sig * (1.0 + pre * (1.0 - sig))).astype(BF16)
    dagg = (dot_nt(w_rel[...], dpre) / count).astype(BF16)
    half = dagg.shape[0] // 2
    for p, out in enumerate(out_daggs):
        out[...] = dagg[p * half : (p + 1) * half]
    flipped = [feats[...].astype(F32).T.astype(BF16), agg_t.astype(BF16)]
    pad = n // tiles * rows - flipped[0].shape[0] - flipped[1].shape[0]
    if pad:
        flipped.append(jnp.zeros((pad, agg_t.shape[1]), BF16))
    lhs = jnp.concatenate(flipped, axis=0)
    for i in range(n // tiles):
        got = dot_nn(lhs[i * rows : (i + 1) * rows], dpre)
        for t in range(tiles):
            at_row = 0
            for out in out_parts:
                size = out.shape[1]
                out[i * tiles + t] = got[at_row : at_row + size, t * LANES : (t + 1) * LANES]
                at_row += size


def adam_kernel(cap, places, rows, seed, daggs, table, m1, m2, o_table, o_m1, o_m2, slot_g, hot):
    size, emb = table.shape
    seeds = daggs[0].shape[2]
    q = LANES // cap
    blocks = rows.shape[0]

    @pl.when(pl.program_id(0) == 0)
    def _():
        for d in range(blocks):
            grads = [
                jnp.concatenate([g[places[p][d * q + k]] for p, g in enumerate(daggs)], axis=0)
                for k in range(q)
            ]
            got = dot_nn(jnp.concatenate(grads, axis=1), seed_hot(seed, d, cap, seeds))
            slot_g[:emb, d * LANES : (d + 1) * LANES] = got.astype(BF16)
        slot_g[emb:, :] = jnp.ones((emb, blocks * LANES), BF16)

    at = lax.broadcasted_iota(I32, (size, LANES), 0) + pl.program_id(0) * size
    for d in range(blocks):
        hot[:, d * LANES : (d + 1) * LANES] = onehot(at == rows[d : d + 1, :])
    got = dot_nt(hot[...], slot_g[...])
    grad, touched = got[:, :emb], got[:, emb:] > 0.5
    m_new = 0.9 * m1[...] + 0.1 * grad
    v_new = 0.999 * m2[...] + 0.001 * grad * grad
    step = 0.05 * (m_new / (1.0 - 0.9**10)) / (jnp.sqrt(v_new / (1.0 - 0.999**10)) + 1e-08)
    o_table[...] = jnp.where(touched, table[...] - step, table[...])
    o_m1[...] = jnp.where(touched, m_new, m1[...])
    o_m2[...] = jnp.where(touched, v_new, m2[...])


def params(**more):
    return pltpu.CompilerParams(vmem_limit_bytes=VMEM_LIMIT, **more)


def grouped(kernel, groups):
    def body(*refs):
        given, at = [], 0
        for k in groups:
            given.append(list(refs[at : at + k]) if k else refs[at])
            at += max(k, 1)
        kernel(*given, *refs[at:])

    return body


def call_grouped(kernel, ins, outs, out_shape, scratch, compiler_params, name):
    count = sum(max(k, 1) for k in ins)
    return pl.pallas_call(
        grouped(kernel, ins + outs),
        out_shape=out_shape,
        in_specs=[VM] * count,
        out_specs=[VM] * len(out_shape),
        scratch_shapes=scratch,
        compiler_params=compiler_params,
        name=name,
    )


def all_to_all(x):
    return lax.all_to_all(x, ("dp", "mp"), split_axis=0, concat_axis=0, tiled=True)


def shards(
    feats,
    edge_owner,
    edge_row,
    counts,
    table,
    moment1,
    moment2,
    w_self,
    w_rel,
    cotangent,
    next_owner,
    next_row,
    paper_table,
):
    n_dp, n_mp = lax.axis_size("dp"), lax.axis_size("mp")
    n = n_dp * n_mp
    orders = orders_of(n_dp, n_mp)
    places = [[position_of(d, n_mp, steps) for d in range(n)] for steps in orders]
    seeds = counts.shape[0]
    edges = edge_row.shape[0]
    n_rows, emb = table.shape
    feat_w, hidden = w_self.shape
    width = paper_table.shape[1]
    cap = max(2, 2 * edges // n)
    fcap = max(2, 2 * seeds // n)
    blocks = n * cap // LANES
    counts_row = counts.reshape(1, seeds)
    shape = jax.ShapeDtypeStruct

    asked_row, asked_seed, asked_paper, paper_place = pl.pallas_call(
        functools.partial(place_kernel, n, cap, fcap, edges // seeds),
        out_shape=[shape((n, cap), I32)] * 2 + [shape((n, fcap), I32), shape((1, seeds), I32)],
        in_specs=[VM] * 5,
        out_specs=[VM] * 4,
        compiler_params=params(),
        name="place",
    )(
        edge_owner.reshape(edges // LANES, LANES),
        edge_row.reshape(edges // LANES, LANES),
        counts_row,
        next_owner.reshape(1, seeds),
        next_row.reshape(1, seeds),
    )

    wanted = all_to_all(jnp.concatenate([asked_row, asked_seed, asked_paper], axis=1))
    rows = wanted[:, :cap].reshape(blocks, LANES)
    slot_seed = wanted[:, cap : 2 * cap].reshape(blocks, LANES)
    answer = pl.pallas_call(
        papers_kernel,
        out_shape=shape((n * fcap, width), BF16),
        in_specs=[VM] * 2,
        out_specs=VM,
        compiler_params=params(),
        name="papers",
    )(wanted[:, 2 * cap :].reshape(n * fcap // LANES, LANES), paper_table)
    paper_rows = all_to_all(answer.reshape(n, fcap, width)).reshape(n * fcap, width)

    sizes = [size for _, size in pieces_of(emb, 4)]
    partial_agg = call_grouped(
        functools.partial(fetch_kernel, cap, places),
        (0, 0, 0),
        (len(sizes),),
        [shape((n, size, seeds), F32) for size in sizes],
        [pltpu.VMEM((2 * emb, n_rows), BF16)],
        params(),
        "fetch",
    )(rows, slot_seed, table)

    narrow = lambda step: step[0] == 0 and step[1] > 1
    scratch = []
    for k, size in enumerate(sizes):
        scratch += rs_scratch(n, (size, seeds), orders[k % 2], narrow)
    agg_sum = call_grouped(
        functools.partial(reduce_kernel, n, orders, narrow),
        (len(sizes),),
        (0,),
        [shape((emb, seeds), F32)],
        scratch,
        params(collective_id=1, has_side_effects=True),
        "sum_agg",
    )(*partial_agg)[0]

    tiles = hidden // LANES
    chunk = -(-(feat_w + emb) * tiles // (n * 16)) * 16
    pieces = pieces_of(chunk, 4)
    out = call_grouped(
        layer_kernel,
        (0,) * 6,
        (4, 2),
        [shape((n, size, LANES), F32) for _, size in pieces]
        + [shape((emb // 2, seeds), BF16)] * 2,
        [],
        params(),
        "layer",
    )(agg_sum, counts_row, feats, w_self, w_rel, cotangent)

    narrow = lambda step: step[0] == 1 or step[1] > 1
    scratch = sems(orders[0]) * 2
    for k, (_, size) in enumerate(pieces):
        scratch += sems(orders[0]) + rs_scratch(n, (size, LANES), orders[k % 2], narrow)
    out = call_grouped(
        functools.partial(exchange_kernel, n, orders, narrow),
        (4, 2),
        (2, 4),
        [shape((n, emb // 2, seeds), BF16)] * 2
        + [shape((n, size, LANES), BF16) for _, size in pieces],
        scratch,
        params(collective_id=2, has_side_effects=True),
        "exchange",
    )(*out)
    daggs, grads = out[:2], out[2:]

    size = min(256, n_rows)
    whole = lambda shape: pl.BlockSpec(shape, lambda i: (0,) * len(shape))
    by_row = pl.BlockSpec((size, emb), lambda i: (i, 0))
    new_table, new_moment1, new_moment2 = pl.pallas_call(
        grouped(functools.partial(adam_kernel, cap, places), (0, 0, 2)),
        out_shape=[shape((n_rows, emb), F32)] * 3,
        grid=(n_rows // size,),
        in_specs=[whole((blocks, LANES))] * 2 + [whole((n, emb // 2, seeds))] * 2 + [by_row] * 3,
        out_specs=[by_row] * 3,
        scratch_shapes=[
            pltpu.VMEM((2 * emb, blocks * LANES), BF16),
            pltpu.VMEM((size, blocks * LANES), BF16),
        ],
        compiler_params=params(),
        name="adam",
    )(rows, slot_seed, *daggs, table, moment1, moment2)

    grad_self, grad_rel, next_feats = call_grouped(
        functools.partial(unpack_kernel, pieces, tiles),
        (4, 0, 0),
        (0, 0, 0),
        [shape((feat_w, hidden), F32), shape((emb, hidden), F32), shape((seeds, width), BF16)],
        [],
        params(),
        "unpack",
    )(*grads, paper_place, paper_rows)
    return (new_table, new_moment1, new_moment2, grad_self, grad_rel, next_feats)


def solution(mesh):
    both = P(("dp", "mp"), None)
    flat = P(("dp", "mp"))
    in_specs = (both, both, flat, flat, both, both, both, P(), P(), both, both, flat, both)
    out_specs = (both, both, both, P(), P(), both)
    return jax.shard_map(shards, mesh=mesh, in_specs=in_specs, out_specs=out_specs, check_vma=False)
```

```python
import functools

import jax
import jax.numpy as jnp
from jax import lax
from jax.experimental import pallas as pl
from jax.experimental.pallas import tpu as pltpu
from jax.sharding import PartitionSpec as P

F32, BF16, I32 = jnp.float32, jnp.bfloat16, jnp.int32
LANES = 128
VMEM_LIMIT = 48 * 1024 * 1024
MESH = pl.DeviceIdType.MESH
VM = pl.BlockSpec(memory_space=pltpu.VMEM)


def dot_nt(a, b):
    return lax.dot_general(a, b, (((1,), (1,)), ((), ())), preferred_element_type=F32)


def dot_nn(a, b):
    return jnp.dot(a, b, preferred_element_type=F32)


def split(x):
    hi = x.astype(BF16)
    return hi, (x - hi.astype(F32)).astype(BF16)


def onehot(mask):
    return jnp.where(mask, 1.0, 0.0).astype(BF16)


def orders_of(n_dp, n_mp):
    core, *chips = [(0, 1 << b) for b in range(n_dp.bit_length() - 1)]
    lines = [(1, 1 << b) for b in range(n_mp.bit_length() - 1)]
    h = len(chips) // 2
    chips = [[*chips, *lines], [*chips[h:], *chips[:h], *lines], [*lines, *chips]]
    return [[core, *order] for order in chips]


def position_of(device, n_mp, steps):
    coords = (device // n_mp, device % n_mp)
    pos = 0
    for axis, w in steps:
        pos = pos * 2 + (coords[axis] // w) % 2
    return pos


def order_at(k):
    return 2 if k == 4 else k % 2


def partners(steps):
    coords = (lax.axis_index("dp"), lax.axis_index("mp"))
    found = []
    for axis, w in steps:
        bit = lax.rem(coords[axis] // w, 2)
        other = coords[axis] + w * (1 - 2 * bit)
        found.append((bit, (other, coords[1]) if axis == 0 else (coords[0], other)))
    return found


def enter(found):
    barrier = pltpu.get_barrier_semaphore()
    for _, device in found:
        pl.semaphore_signal(barrier, inc=1, device_id=device, device_id_type=MESH)
    pl.semaphore_wait(barrier, len(found))


def my_position(found):
    pos = 0
    for bit, _ in found:
        pos = pos * 2 + bit
    return pos


def pieces_of(rows, count):
    groups, at, found = rows // 16, 0, []
    for i in range(count):
        size = (groups // count + (i < groups % count)) * 16
        found.append((at, size))
        at += size
    return found


def sems(steps):
    return [pltpu.SemaphoreType.DMA((len(steps),)) for _ in range(2)]


def rs_scratch(n, block, steps, narrow):
    shapes = sems(steps)
    for s, step in enumerate(steps):
        half = n >> (s + 1)
        shapes += [pltpu.VMEM((half, *block), BF16 if narrow(step) else F32)]
        shapes += [pltpu.VMEM((half, *block), F32)]
        shapes += [pltpu.VMEM((half, *block) if narrow(step) else (1, 16, LANES), BF16)]
    return shapes


def rs_chain(x, n, steps, found, narrow, scratch):
    send, recv = scratch[:2]
    cur = x
    for s, (bit, device) in enumerate(found):
        half = n >> (s + 1)
        arrive, total, rounded = scratch[2 + 3 * s : 5 + 3 * s]
        away, keep = (1 - bit) * half, bit * half
        src = cur.at[pl.ds(away, half)]
        if narrow(steps[s]):
            src = rounded

            @pl.loop(0, half)
            def _(i, cur=cur, rounded=rounded, away=away):
                rounded[i] = cur[away + i].astype(BF16)

        copy = pltpu.make_async_remote_copy(
            src_ref=src, dst_ref=arrive, send_sem=send.at[s], recv_sem=recv.at[s],
            device_id=device, device_id_type=MESH,
        )
        copy.start()
        yield
        copy.wait()

        @pl.loop(0, half)
        def _(i, cur=cur, total=total, arrive=arrive, keep=keep):
            total[i] = cur[keep + i] + arrive[i].astype(F32)

        cur = total
    return cur


def ag_chain(out, n, found, scratch):
    send, recv = scratch
    pos = my_position(found)
    for s in reversed(range(len(found))):
        size = n >> (s + 1)
        here = out.at[pl.ds((pos // size) * size, size)]
        copy = pltpu.make_async_remote_copy(
            src_ref=here, dst_ref=here, send_sem=send.at[s], recv_sem=recv.at[s],
            device_id=found[s][1], device_id_type=MESH,
        )
        copy.start()
        yield
        copy.wait()


def run(chains):
    while chains:
        left = []
        for chain in chains:
            try:
                next(chain)
                left.append(chain)
            except StopIteration:
                pass
        chains = left


def reduce_kernel(n, orders, narrow, xs, out, *scratch):
    found = [partners(steps) for steps in orders]
    enter(found[0])
    per = len(scratch) // len(xs)
    starts = [0]
    for x in xs:
        starts.append(starts[-1] + x.shape[1])

    def chain(k):
        mine = scratch[k * per : (k + 1) * per]
        total = yield from rs_chain(xs[k], n, orders[k % 2], found[k % 2], narrow, mine)
        out[starts[k] : starts[k + 1], :] = total[0]

    run([chain(k) for k in range(len(xs))])


def exchange_kernel(
    n, orders, narrow, cap, places, parts, daggs, rows, seed, out_got, out_grads, *scratch
):
    found = [partners(steps) for steps in orders]
    pos = [my_position(f) for f in found]
    enter(found[0])
    count, small = len(parts), 2 * len(daggs)
    slot_g, hot, *arrived = scratch[: 2 + len(daggs)]
    scratch = scratch[2 + len(daggs) :]
    mine, rest = scratch[:small], scratch[small:]
    per = len(rest) // count

    def row_chain(k):
        arrived[k][pos[k % 2]] = daggs[k][...]
        yield from ag_chain(arrived[k], n, found[k % 2], mine[2 * k : 2 * k + 2])

    def grad_chain(k):
        own = rest[k * per : (k + 1) * per]
        at = order_at(k)
        total = yield from rs_chain(parts[k], n, orders[at], found[at], narrow, own[2:])
        out_grads[k][pos[at]] = total[0].astype(BF16)
        yield from ag_chain(out_grads[k], n, found[at], own[:2])

    def row_grads():
        for _ in orders[0]:
            yield
        blocks, size = rows.shape[0], hot.shape[0]
        emb = slot_g.shape[0] // 2
        seeds = arrived[0].shape[2]
        q = LANES // cap
        for d in range(blocks):
            grads = [
                jnp.concatenate([g[places[p][d * q + k]] for p, g in enumerate(arrived)], axis=0)
                for k in range(q)
            ]
            got = dot_nn(jnp.concatenate(grads, axis=1), seed_hot(seed, d, cap, seeds))
            slot_g[:emb, d * LANES : (d + 1) * LANES] = got.astype(BF16)
        slot_g[emb:, :] = jnp.ones((emb, blocks * LANES), BF16)
        for first in range(0, out_got.shape[0], size):
            yield
            at = lax.broadcasted_iota(I32, (size, LANES), 0) + first
            for d in range(blocks):
                hot[:, d * LANES : (d + 1) * LANES] = onehot(at == rows[d : d + 1, :])
            out_got[first : first + size, :] = dot_nt(hot[...], slot_g[...])

    chains = [grad_chain(k) for k in range(count)] + [row_chain(k) for k in range(len(daggs))]
    run(chains + [row_grads()])


def place_kernel(
    n, cap, fcap, slots_per, given, out_row, out_seed, out_asked, out_place, held, arrived
):
    copies = [
        pltpu.make_async_copy(src, dst, arrived.at[i])
        for i, (src, dst) in enumerate(zip(given, held))
    ]
    for copy in copies:
        copy.start()
    for copy in copies:
        copy.wait()
    owner, row, counts, p_owner, p_row = held
    blocks = owner.shape[0]
    seeds = counts.shape[1]
    per = LANES // slots_per
    at_seed = lax.broadcasted_iota(I32, (blocks, seeds), 1)
    at_block = lax.broadcasted_iota(I32, (blocks, seeds), 0)
    spread = jnp.where(at_seed // per == at_block, counts[...].astype(F32), 0.0).astype(BF16)
    s_i = lax.broadcasted_iota(I32, (seeds, LANES), 0)
    l_i = lax.broadcasted_iota(I32, (seeds, LANES), 1)
    count = dot_nn(spread, onehot(lax.rem(s_i, per) == l_i // slots_per))
    lane = lax.broadcasted_iota(I32, (blocks, LANES), 1)
    live = lax.rem(lane, slots_per).astype(F32) < count - 0.5
    wanted = jnp.where(live, row[...] + 1, 0)
    seed = lax.broadcasted_iota(I32, (blocks, LANES), 0) * per + lane // slots_per
    parts = [(wanted // 64).astype(F32), lax.rem(wanted, 64).astype(F32), seed.astype(F32)]
    dev = lax.broadcasted_iota(I32, (n, LANES), 0)
    hot = [jnp.where(dev == owner[a : a + 1, :], 1.0, 0.0) for a in range(blocks)]
    t_i = lax.broadcasted_iota(I32, (LANES, LANES), 0)
    t_j = lax.broadcasted_iota(I32, (LANES, LANES), 1)
    before = dot_nn(jnp.concatenate([h.astype(BF16) for h in hot], axis=0), onehot(t_i < t_j))
    base = jnp.zeros((n, 1), F32)
    place = lax.broadcasted_iota(I32, (cap, LANES), 0).astype(F32)
    left, right = [], []
    for a in range(blocks):
        slot = jnp.sum(hot[a] * (before[a * n : (a + 1) * n] + base), axis=0, keepdims=True)
        base = base + jnp.sum(hot[a], axis=1, keepdims=True)
        right.append(onehot(place == slot))
        left.append(
            jnp.concatenate([(hot[a] * p[a : a + 1, :]).astype(BF16) for p in parts], axis=0)
        )
    got = dot_nt(jnp.concatenate(left, axis=1), jnp.concatenate(right, axis=1))
    out_row[...] = (got[:n] * 64.0 + got[n : 2 * n] - 1.0).astype(I32)
    out_seed[...] = got[2 * n :].astype(I32)
    p_hot = jnp.where(dev == p_owner[...], 1.0, 0.0)
    slot = jnp.sum(p_hot * dot_nn(p_hot.astype(BF16), onehot(t_i < t_j)), axis=0, keepdims=True)
    out_place[...] = p_owner[...] * fcap + slot.astype(I32)
    high, low = p_row[...] // 64, lax.rem(p_row[...], 64)
    pair = [(p_hot * v.astype(F32)).astype(BF16) for v in (high, low)]
    at_slot = onehot(lax.broadcasted_iota(I32, (fcap, LANES), 0).astype(F32) == slot)
    got = dot_nt(jnp.concatenate(pair, axis=0), at_slot)
    out_asked[...] = (got[:n] * 64.0 + got[n:]).astype(I32)


def pick(rows, wanted):
    at = lax.broadcasted_iota(I32, (rows.shape[0], LANES), 0)
    got = [
        lax.dot_general(
            onehot(at == wanted[i : i + 1, :]), rows, (((0,), (0,)), ((), ())),
            preferred_element_type=F32,
        )
        for i in range(wanted.shape[0])
    ]
    return jnp.concatenate(got, axis=0).astype(BF16)


def papers_kernel(wanted, papers, out):
    out[...] = pick(papers[...], wanted)


def unpack_kernel(pieces, tiles, grads, place, rows, out_self, out_rel, out_next):
    out_next[...] = pick(rows[...], place)
    chunk = sum(size for _, size in pieces)
    for (start, size), grad in zip(pieces, grads):
        for j in range(grad.shape[0]):
            top = j // tiles * chunk + start
            cols = slice(j % tiles * LANES, (j % tiles + 1) * LANES)
            first = 0
            for out in (out_self, out_rel):
                low, high = max(top, first), min(top + size, first + out.shape[0])
                if low < high:
                    out[low - first : high - first, cols] = grad[j, low - top : high - top].astype(F32)
                first += out.shape[0]


def seed_hot(seed, d, cap, seeds):
    q = LANES // cap
    lane = lax.broadcasted_iota(I32, (1, LANES), 1)
    which = seed[pl.ds(d, 1), :] + seeds * (lane // cap)
    return onehot(lax.broadcasted_iota(I32, (q * seeds, LANES), 0) == which)


def fetch_kernel(cap, places, rows, seed, table, outs, packed, hot):
    n_rows, emb = table.shape
    seeds = sum(out.shape[1] for out in outs)
    blocks = rows.shape[0]
    q = LANES // cap
    hi, lo = split(table[...])
    packed[:, :emb] = hi
    packed[:, emb:] = lo
    number = jnp.concatenate(
        [rows[...].astype(F32), jnp.zeros((LANES - blocks, LANES), F32)], axis=0
    ).T.astype(I32)
    at = lax.broadcasted_iota(I32, (LANES, n_rows), 1)
    group = hot.shape[0] // LANES
    for first in range(0, blocks, group):
        for j in range(group):
            d = first + j
            hot[j * LANES : (j + 1) * LANES, :] = onehot(at == number[:, d : d + 1])
        got = dot_nn(hot[...], packed[...])
        vals = got[:, :emb] + got[:, emb:]
        for j in range(group):
            d = first + j
            pair = jnp.concatenate(split(vals[j * LANES : (j + 1) * LANES]), axis=1)
            both = dot_nn(seed_hot(seed, d, cap, seeds), pair)
            sums = both[:, :emb] + both[:, emb:]
            for k in range(q):
                at_row = k * seeds
                for p, out in enumerate(outs):
                    size = out.shape[1]
                    out[places[p % 2][d * q + k]] = sums[at_row : at_row + size]
                    at_row += size


def layer_kernel(agg_sum, counts, feats, w_self, w_rel, cot, out_parts, out_daggs):
    n = out_parts[0].shape[0]
    rows = sum(out.shape[1] for out in out_parts)
    width = w_self.shape[1]
    tiles = width // LANES
    count = counts[...].astype(F32)
    agg_t = agg_sum[...].T / count
    agg_b = agg_t.T.astype(BF16)
    pre = dot_nn(feats[...], w_self[...]) + dot_nn(agg_b, w_rel[...])
    sig = 1.0 / (1.0 + jnp.exp(-pre))
    dpre = (cot[...] * sig * (1.0 + pre * (1.0 - sig))).astype(BF16)
    dagg = (dot_nt(w_rel[...], dpre) / count).astype(BF16)
    half = dagg.shape[0] // 2
    for p, out in enumerate(out_daggs):
        out[...] = dagg[p * half : (p + 1) * half]
    flipped = [feats[...].astype(F32).T.astype(BF16), agg_t.astype(BF16)]
    pad = n // tiles * rows - flipped[0].shape[0] - flipped[1].shape[0]
    if pad:
        flipped.append(jnp.zeros((pad, agg_t.shape[1]), BF16))
    lhs = jnp.concatenate(flipped, axis=0)
    for i in range(n // tiles):
        got = dot_nn(lhs[i * rows : (i + 1) * rows], dpre)
        for t in range(tiles):
            at_row = 0
            for out in out_parts:
                size = out.shape[1]
                out[i * tiles + t] = got[at_row : at_row + size, t * LANES : (t + 1) * LANES]
                at_row += size


def adam_kernel(got, table, m1, m2, o_table, o_m1, o_m2):
    emb = table.shape[1]
    grad, touched = got[:, :emb], got[:, emb:] > 0.5
    m_new = 0.9 * m1[...] + 0.1 * grad
    v_new = 0.999 * m2[...] + 0.001 * grad * grad
    step = 0.05 * (m_new / (1.0 - 0.9**10)) / (jnp.sqrt(v_new / (1.0 - 0.999**10)) + 1e-08)
    o_table[...] = jnp.where(touched, table[...] - step, table[...])
    o_m1[...] = jnp.where(touched, m_new, m1[...])
    o_m2[...] = jnp.where(touched, v_new, m2[...])


def params(**more):
    return pltpu.CompilerParams(vmem_limit_bytes=VMEM_LIMIT, **more)


def grouped(kernel, groups):
    def body(*refs):
        given, at = [], 0
        for k in groups:
            given.append(list(refs[at : at + k]) if k else refs[at])
            at += max(k, 1)
        kernel(*given, *refs[at:])

    return body


def call_grouped(kernel, ins, outs, out_shape, scratch, compiler_params, name):
    count = sum(max(k, 1) for k in ins)
    return pl.pallas_call(
        grouped(kernel, ins + outs),
        out_shape=out_shape,
        in_specs=[VM] * count,
        out_specs=[VM] * len(out_shape),
        scratch_shapes=scratch,
        compiler_params=compiler_params,
        name=name,
    )


def all_to_all(x):
    return lax.all_to_all(x, ("dp", "mp"), split_axis=0, concat_axis=0, tiled=True)


def shards(
    feats,
    edge_owner,
    edge_row,
    counts,
    table,
    moment1,
    moment2,
    w_self,
    w_rel,
    cotangent,
    next_owner,
    next_row,
    paper_table,
):
    n_dp, n_mp = lax.axis_size("dp"), lax.axis_size("mp")
    n = n_dp * n_mp
    orders = orders_of(n_dp, n_mp)
    places = [[position_of(d, n_mp, steps) for d in range(n)] for steps in orders]
    seeds = counts.shape[0]
    edges = edge_row.shape[0]
    n_rows, emb = table.shape
    feat_w, hidden = w_self.shape
    width = paper_table.shape[1]
    cap = max(2, 2 * edges // n)
    fcap = max(2, 2 * seeds // n)
    blocks = n * cap // LANES
    counts_row = counts.reshape(1, seeds)
    shape = jax.ShapeDtypeStruct

    given = [x.reshape(edges // LANES, LANES) for x in (edge_owner, edge_row)]
    given += [counts_row, next_owner.reshape(1, seeds), next_row.reshape(1, seeds)]
    asked_row, asked_seed, asked_paper, paper_place = pl.pallas_call(
        grouped(
            functools.partial(place_kernel, n, cap, fcap, edges // seeds),
            (len(given), 0, 0, 0, 0, len(given)),
        ),
        out_shape=[shape((n, cap), I32)] * 2 + [shape((n, fcap), I32), shape((1, seeds), I32)],
        in_specs=[pl.BlockSpec(memory_space=pl.ANY)] * len(given),
        out_specs=[VM] * 4,
        scratch_shapes=[pltpu.VMEM(x.shape, I32) for x in given]
        + [pltpu.SemaphoreType.DMA((len(given),))],
        compiler_params=pltpu.CompilerParams(vmem_limit_bytes=60 * 1024 * 1024),
        name="place",
    )(*given)

    wanted = all_to_all(jnp.concatenate([asked_row, asked_seed, asked_paper], axis=1))
    rows = wanted[:, :cap].reshape(blocks, LANES)
    slot_seed = wanted[:, cap : 2 * cap].reshape(blocks, LANES)
    answer = pl.pallas_call(
        papers_kernel,
        out_shape=shape((n * fcap, width), BF16),
        in_specs=[VM] * 2,
        out_specs=VM,
        compiler_params=params(),
        name="papers",
    )(wanted[:, 2 * cap :].reshape(n * fcap // LANES, LANES), paper_table)
    paper_rows = all_to_all(answer.reshape(n, fcap, width)).reshape(n * fcap, width)

    sizes = [size for _, size in pieces_of(seeds, 4)]
    partial_agg = call_grouped(
        functools.partial(fetch_kernel, cap, places),
        (0, 0, 0),
        (len(sizes),),
        [shape((n, size, emb), F32) for size in sizes],
        [pltpu.VMEM((n_rows, 2 * emb), BF16), pltpu.VMEM((8 * LANES, n_rows), BF16)],
        params(),
        "fetch",
    )(rows, slot_seed, table)

    narrow = lambda step: step[0] == 0 and step[1] > 1
    scratch = []
    for k, size in enumerate(sizes):
        scratch += rs_scratch(n, (size, emb), orders[k % 2], narrow)
    agg_sum = call_grouped(
        functools.partial(reduce_kernel, n, orders, narrow),
        (len(sizes),),
        (0,),
        [shape((seeds, emb), F32)],
        scratch,
        params(collective_id=1, has_side_effects=True),
        "sum_agg",
    )(*partial_agg)[0]

    tiles = hidden // LANES
    chunk = -(-(feat_w + emb) * tiles // (n * 16)) * 16
    pieces = pieces_of(chunk, min(5, chunk // 16))
    out = call_grouped(
        layer_kernel,
        (0,) * 6,
        (len(pieces), 2),
        [shape((n, size, LANES), F32) for _, size in pieces]
        + [shape((emb // 2, seeds), BF16)] * 2,
        [],
        params(),
        "layer",
    )(agg_sum, counts_row, feats, w_self, w_rel, cotangent)

    narrow = lambda step: step[0] == 1 or step[1] > 1
    size = min(512, n_rows)
    scratch = [pltpu.VMEM((2 * emb, blocks * LANES), BF16), pltpu.VMEM((size, blocks * LANES), BF16)]
    scratch += [pltpu.VMEM((n, emb // 2, seeds), BF16)] * 2 + sems(orders[0]) * 2
    for k, (_, height) in enumerate(pieces):
        scratch += sems(orders[0]) + rs_scratch(n, (height, LANES), orders[order_at(k)], narrow)
    got, *grads = call_grouped(
        functools.partial(exchange_kernel, n, orders, narrow, cap, places),
        (len(pieces), 2, 0, 0),
        (0, len(pieces)),
        [shape((n_rows, 2 * emb), F32)]
        + [shape((n, height, LANES), BF16) for _, height in pieces],
        scratch,
        params(collective_id=2, has_side_effects=True),
        "exchange",
    )(*out, rows, slot_seed)

    by_row = lambda wide: pl.BlockSpec((size, wide), lambda i: (i, 0))
    new_table, new_moment1, new_moment2 = pl.pallas_call(
        adam_kernel,
        out_shape=[shape((n_rows, emb), F32)] * 3,
        grid=(n_rows // size,),
        in_specs=[by_row(2 * emb)] + [by_row(emb)] * 3,
        out_specs=[by_row(emb)] * 3,
        compiler_params=params(),
        name="adam",
    )(got, table, moment1, moment2)

    grad_self, grad_rel, next_feats = call_grouped(
        functools.partial(unpack_kernel, pieces, tiles),
        (len(pieces), 0, 0),
        (0, 0, 0),
        [shape((feat_w, hidden), F32), shape((emb, hidden), F32), shape((seeds, width), BF16)],
        [],
        params(),
        "unpack",
    )(*grads, paper_place, paper_rows)
    return (new_table, new_moment1, new_moment2, grad_self, grad_rel, next_feats)


def solution(mesh):
    both = P(("dp", "mp"), None)
    flat = P(("dp", "mp"))
    in_specs = (both, both, flat, flat, both, both, both, P(), P(), both, both, flat, both)
    out_specs = (both, both, both, P(), P(), both)
    return jax.shard_map(shards, mesh=mesh, in_specs=in_specs, out_specs=out_specs, check_vma=False)
```
